32 devices in a mesh: dp: 2 (over core), expert: 16 (over z, y, x).
Axes of the slice: x: 2, y: 2, z: 4, core: 2. Of those that a mesh axis runs over, the one named last changes fastest.
Arguments:
- tokens: bfloat16 [384, 5120], P(('dp', 'expert')), may hold values from -6 to 6
- router_weight: bfloat16 [384], P(('dp', 'expert')), may hold values from 0.19921875 to 1
- initial_id: int32 [384, 1], P(('dp', 'expert')), may hold values from 0 to 3; in each aligned block of 192 rows (0 to 191, 192 to 383, ...) at most 80 rows name the same one
- group_map: int32 [4], replicated, may hold values from 0 to 1, as said below
- teacher_gate: bfloat16 [5120, 16384], P(None, 'expert'), may hold values from -0.078125 to 0.078125
- teacher_up: bfloat16 [5120, 16384], P(None, 'expert'), may hold values from -0.078125 to 0.078125
- teacher_down: bfloat16 [16384, 5120], P('expert'), may hold values from -0.09375 to 0.09375
- student_gate: bfloat16 [5120, 8192], P(None, 'expert'), may hold values from -0.078125 to 0.078125
- student_up: bfloat16 [5120, 8192], P(None, 'expert'), may hold values from -0.078125 to 0.078125
- student_down: bfloat16 [8192, 5120], P('expert'), may hold values from -0.09375 to 0.09375
Outputs:
- grad_gate: float32 [5120, 8192], P('dp', 'expert')
- grad_up: float32 [5120, 8192], P('dp', 'expert')
- grad_down: float32 [8192, 5120], P('expert', 'dp')
The draws below stay inside these ranges and needn't reach their ends.
Inputs may be any that keep to these rules, and one draw needn't show every extreme that they name: `initial_id`: in each half of the tokens (rows h * 12 * 16 to (h + 1) * 12 * 16 - 1, h = 0, 1) every initial expert is named by at most 80 tokens, and some expert of some half by exactly 80. `group_map`: every merged expert is named by exactly 2 entries.
All inputs are finite; a program needn't handle non-finite values.
Results may differ from the reference program's by a relative error of at most 0.013.
Values may be sent and summed in bfloat16 or wider, within the bound.
A program may use at most 192 MiB of HBM per device.

```python
import math
import jax
import jax.numpy as jnp
import numpy as np

D = 5120
F = 4096
E_ORIG = 4
GROUP = 2
E_MERGE = 2
TOK_DEV = 12
TOKENS = 384
CAP = 80
N_EXPERT = 16


def draw_group_map(key, part):
    key = jax.random.fold_in(key, 7)
    return (jax.random.permutation(key, E_ORIG) // GROUP).astype(jnp.int32)


def steps_of(own_key, shape, cuts, least, top_value):
    loudness, own = 1.0, jax.random.fold_in(own_key, 6)
    for axis_at, blocks in cuts:
        heights = jnp.exp(jax.random.uniform(jax.random.fold_in(own, axis_at), (blocks,), jnp.float32, least / len(cuts), top_value / len(cuts)))
        loudness = loudness * jnp.repeat(heights, shape[axis_at] // blocks).reshape([-1 if axis == axis_at else 1 for axis in range(len(shape))])
    return loudness


def routed_block(stream_key, own, number, rows, amount, top, bound, lean):
    sequence = jax.random.permutation(stream_key, amount)
    packed, common = portions_of(amount, rows * top, bound, lean, True), portions_of(amount, rows * top, bound, lean, False)
    places = jnp.arange(amount)

    def named(sizes, rotation):
        used = int((sizes > 0).sum())
        fixed = max(1, used // 4)
        shifted = fixed + (places - fixed + rotation * (used - fixed)) % max(1, amount - fixed)
        return jnp.zeros((amount,), jnp.int32).at[sequence[jnp.where(places < fixed, places, shifted)]].set(jnp.asarray(sizes, jnp.int32))

    sizes = jnp.where(number % 4 == 0, named(packed, number // 4), named(common, number - number // 4 - 1))
    mixed = jax.random.permutation(jax.random.fold_in(own, 3), amount)
    giver, sink = mixed[0:amount // 2 * 2:2], mixed[1:amount // 2 * 2:2]
    slack = jnp.minimum(sizes[giver] - 1, bound - sizes[sink]) // 2
    slack = jnp.where((giver == sequence[0]) | (sink == sequence[0]) | (sizes[sink] == 0), 0, jnp.maximum(slack, 0))
    shifted = jax.random.randint(jax.random.fold_in(own, 4), (amount // 2,), 0, 1 << 20) % (slack + 1)
    sizes = sizes.at[giver].add(-shifted).at[sink].add(shifted)
    members = jnp.searchsorted(jnp.cumsum(sizes), jnp.arange(rows * top), side="right").astype(jnp.int32)
    grid = members.reshape(top, rows).T
    grid = grid[jax.random.permutation(jax.random.fold_in(own, 1), rows)]
    rotation = jax.random.randint(jax.random.fold_in(own, 2), (rows, 1), 0, top)
    return jnp.take_along_axis(grid, (jnp.arange(top)[None, :] + rotation) % top, axis=1)


def portions_of(amount, total, bound, slope, full):
    portions = [(1 << 20) // math.isqrt(standing ** slope) + 1 for standing in range(1, amount + 1)]
    largest = bound if full else min(bound, max(-(-total // amount), total * portions[0] // sum(portions)))
    least = 1 if total - largest >= amount - 1 else 0
    counts, rest = [largest] + [least] * (amount - 1), total - largest - least * (amount - 1)
    while rest > 0:
        movable = [i for i in range(1, amount) if counts[i] < largest] or [i for i in range(1, amount) if counts[i] < bound]
        whole, left = sum([portions[i] for i in movable]), rest
        for i in movable:
            extra = min(bound - counts[i], max(1, left * portions[i] // whole), rest)
            counts[i] = counts[i] + extra
            rest = rest - extra
    return np.array(counts)


def noise(key, shape, deviation, reach, shards=(), kind=jnp.bfloat16):
    factor_of = steps_of(key, shape, shards, -0.22, 0.18) if shards else 1.0
    result = jax.random.normal(key, shape, jnp.float32) * deviation * factor_of
    return jnp.minimum(jnp.maximum(result, -reach), reach).astype(kind)


def setup_inputs(seed: int = 0) -> dict:
    arg_keys = jax.random.split(jax.random.key(seed), 11)
    tokens = noise(arg_keys[0], (TOKENS, D), 1.0, 6.0, ((0, 32),))
    router_weight = jnp.clip(0.19921875 + 0.80078125 * jax.random.uniform(arg_keys[1], (TOKENS,), jnp.float32) ** steps_of(arg_keys[1], (TOKENS,), ((0, 32),), -0.2, 0.2), 0.19921875, 1.0).astype(jnp.bfloat16)
    initial_id_keys = jax.random.split(jax.random.fold_in(arg_keys[2], 1), TOKENS // (TOK_DEV * N_EXPERT))
    initial_id_turns = jax.random.permutation(jax.random.fold_in(arg_keys[2], 3), TOKENS // (TOK_DEV * N_EXPERT))
    initial_id = jax.vmap(lambda own, number: routed_block(jax.random.fold_in(arg_keys[2], 2), own, number, TOK_DEV * N_EXPERT, E_ORIG, 1, CAP, 1))(initial_id_keys, initial_id_turns).reshape((TOKENS, 1))
    group_map = draw_group_map(jax.random.fold_in(arg_keys[10], 71), 0)
    teacher_gate = noise(arg_keys[4], (D, E_ORIG * F), D ** -0.5, 0.078125, ((1, 16),))
    teacher_up = noise(arg_keys[5], (D, E_ORIG * F), D ** -0.5, 0.078125, ((1, 16),))
    teacher_down = noise(arg_keys[6], (E_ORIG * F, D), F ** -0.5, 0.09375, ((0, 16),))
    student_gate = noise(arg_keys[7], (D, E_MERGE * F), D ** -0.5, 0.078125, ((1, 16),))
    student_up = noise(arg_keys[8], (D, E_MERGE * F), D ** -0.5, 0.078125, ((1, 16),))
    student_down = noise(arg_keys[9], (E_MERGE * F, D), F ** -0.5, 0.09375, ((0, 16),))
    return dict(tokens=tokens, router_weight=router_weight, initial_id=initial_id, group_map=group_map, teacher_gate=teacher_gate, teacher_up=teacher_up, teacher_down=teacher_down, student_gate=student_gate, student_up=student_up, student_down=student_down)


def expert_forward(rows, w_gate, w_up):
    gate = jnp.dot(rows, w_gate, preferred_element_type=jnp.float32)
    upper = jnp.dot(rows, w_up, preferred_element_type=jnp.float32)
    hidden = (jax.nn.silu(gate) * upper).astype(jnp.bfloat16)
    return (gate, upper, hidden)

def reference(tokens, router_weight, initial_id, group_map, teacher_gate, teacher_up, teacher_down, student_gate, student_up, student_down):
    ids = initial_id[:, 0]
    weight = router_weight.astype(jnp.float32)
    teacher = jnp.zeros((TOKENS, D), jnp.float32)
    for orig in range(E_ORIG):
        cols = slice(orig * F, (orig + 1) * F)
        gate, upper, hidden = expert_forward(tokens, teacher_gate[:, cols], teacher_up[:, cols])
        out_rows = jnp.dot(hidden, teacher_down[cols, :], preferred_element_type=jnp.float32)
        teacher = jnp.where((ids == orig)[:, None], out_rows, teacher)
    merged_of = group_map[ids]
    student = jnp.zeros((TOKENS, D), jnp.float32)
    saved = []
    for merged in range(E_MERGE):
        cols = slice(merged * F, (merged + 1) * F)
        gate, upper, hidden = expert_forward(tokens, student_gate[:, cols], student_up[:, cols])
        out_rows = jnp.dot(hidden, student_down[cols, :], preferred_element_type=jnp.float32)
        student = jnp.where((merged_of == merged)[:, None], out_rows, student)
        saved.append((gate, upper, hidden))
    mismatch = weight[:, None] * (student - teacher)
    cotangent = (weight[:, None] * mismatch / math.sqrt(TOKENS)).astype(jnp.bfloat16)
    gate_parts, up_parts, down_parts = ([], [], [])
    for merged in range(E_MERGE):
        cols = slice(merged * F, (merged + 1) * F)
        gate, upper, hidden = saved[merged]
        chosen = jnp.where((merged_of == merged)[:, None], cotangent, jnp.zeros_like(cotangent))
        dhidden = jnp.dot(chosen, student_down[cols, :].T, preferred_element_type=jnp.float32)
        sigma = jax.nn.sigmoid(gate)
        dgate = (dhidden * upper * sigma * (1.0 + gate * (1.0 - sigma))).astype(jnp.bfloat16)
        dup = (dhidden * jax.nn.silu(gate)).astype(jnp.bfloat16)
        gate_parts.append(jnp.dot(tokens.T, dgate, preferred_element_type=jnp.float32))
        up_parts.append(jnp.dot(tokens.T, dup, preferred_element_type=jnp.float32))
        down_parts.append(jnp.dot(hidden.T, chosen, preferred_element_type=jnp.float32))
    return (jnp.concatenate(gate_parts, axis=1), jnp.concatenate(up_parts, axis=1), jnp.concatenate(down_parts, axis=0))
```

```python
import functools
import math

import jax
import jax.numpy as jnp
from jax import lax
from jax.experimental import pallas as pl
from jax.experimental.pallas import tpu as pltpu
from jax.sharding import PartitionSpec as P

F = 4096
SLOT = 16
EXTRA = 128
MESH = pl.DeviceIdType.MESH
Y, X, Z = 0, 1, 2
ORDERS = ((Z, X, Y), (Z, Y, X), (Z, X, Y), (Z, Y, X))
bf16, f32 = jnp.bfloat16, jnp.float32


def bounds_of(width):
    step = width // 128 // len(ORDERS) * 128
    edges = [step * i for i in range(len(ORDERS))] + [width]
    return list(zip(edges[:-1], edges[1:]))


def kernel(sizes, tok, width, *refs):
    (x_ref, tg_h, tu_h, td_h, sg_h, su_h, sd_h) = refs[:7]
    (got_gate, got_up, got_down, xg_o, cot_o, dg_o, du_o, sh_o) = refs[7:15]
    (tg, tu, td, sg, su, sd, xg, part, cot, gate, up, th, sh, dg, du) = refs[15:30]
    (w_sem, o_sem, g_send, g_recv, a_send, a_recv, c_send, c_recv, r_send, r_recv) = refs[30:40]
    rbufs = refs[40:]
    sy, sx, sz = sizes
    count = sy * sx * sz
    rows = count * SLOT
    y_tile = max(1, 256 // (sx * sz * SLOT))
    m_rows = y_tile * sx * sz * SLOT
    m_steps = sy // y_tile
    tw, sw = tg.shape[1], sg.shape[1]
    half = width // 2

    me = lax.axis_index("expert")
    core = lax.axis_index("dp")
    at = [lax.rem(me // sx, sy), lax.rem(me, sx), me // (sx * sy)]

    def number(pos):
        return (pos[Z] * sy + pos[Y]) * sx + pos[X]

    def moved(axis, k):
        pos = list(at)
        pos[axis] = lax.rem(at[axis] + k + sizes[axis], sizes[axis])
        return pos

    loads = []
    for i, (src, dst) in enumerate(
        ((tg_h, tg), (tu_h, tu), (sg_h, sg), (su_h, su), (td_h, td), (sd_h, sd))
    ):
        loads.append(pltpu.make_async_copy(src, dst, w_sem.at[i]))

    barrier = pltpu.get_barrier_semaphore()
    for axis in (Y, X, Z):
        for k in range(1, sizes[axis]):
            pl.semaphore_signal(
                barrier, inc=1, device_id={"expert": number(moved(axis, k))}, device_id_type=MESH
            )
    pl.semaphore_signal(barrier, inc=1, device_id={"dp": 1 - core}, device_id_type=MESH)
    xg[pl.ds(at[Y], 1), pl.ds(at[X], 1), pl.ds(at[Z], 1)] = x_ref[...].reshape(1, 1, 1, SLOT, -1)
    pl.semaphore_wait(barrier, sy + sx + sz - 2)

    def region(pos, done):
        return tuple(
            pl.ds(0, sizes[a]) if a in done else pl.ds(pos[a], 1) for a in (Y, X, Z)
        )

    def view(ref, pos, done, cols):
        return ref.at[region(pos, done) + (pl.ds(0, SLOT), pl.ds(cols[0], cols[1] - cols[0]))]

    def spread(buf, send, recv, c, cols, stage):
        axis, done = ORDERS[c][stage], ORDERS[c][:stage]
        copies = []
        for k in range(1, sizes[axis]):
            mine = view(buf, at, done, cols)
            out = pltpu.make_async_remote_copy(
                src_ref=mine, dst_ref=mine,
                send_sem=send.at[c, stage, k - 1], recv_sem=recv.at[c, stage, k - 1],
                device_id={"expert": number(moved(axis, k))}, device_id_type=MESH,
            )
            theirs = view(buf, moved(axis, -k), done, cols)
            came = pltpu.make_async_remote_copy(
                src_ref=theirs, dst_ref=theirs,
                send_sem=send.at[c, stage, k - 1], recv_sem=recv.at[c, stage, k - 1],
                device_id={"expert": number(moved(axis, -k))}, device_id_type=MESH,
            )
            copies.append((out, came))
        return copies

    def begin(copies):
        for out, _ in copies:
            out.start()

    def arrive(copies):
        for _, came in copies:
            came.wait_recv()

    def left(copies):
        for out, _ in copies:
            out.wait_send()

    x_cols = bounds_of(width + EXTRA)
    plan = [[spread(xg, a_send, a_recv, c, x_cols[c], s) for s in range(3)] for c in range(len(ORDERS))]
    for c in range(len(ORDERS)):
        begin(plan[c][0])
    for load in loads:
        load.start()
    for s in (1, 2):
        for c in range(len(ORDERS)):
            arrive(plan[c][s - 1])
            begin(plan[c][s])
    for c in range(len(ORDERS)):
        arrive(plan[c][2])
    outs = [pltpu.make_async_copy(xg, xg_o, o_sem.at[0])]
    outs[0].start()

    def tile_of(ref, m, cols):
        got = ref[pl.ds(m * y_tile, y_tile), :, :, :, cols]
        return got.reshape(m_rows, got.shape[-1])

    def row_ds(m):
        return pl.ds(pl.multiple_of(m * m_rows, m_rows), m_rows)

    def facts(m):
        extra = tile_of(xg, m, pl.ds(width, EXTRA)).astype(f32)
        weight, ids, merged = extra[:, 0:1], extra[:, 1:2], extra[:, 2:3]
        t_own = (me * tw // F).astype(f32)
        s_own = (me * sw // F).astype(f32)
        return (
            jnp.where(ids == t_own, -weight, 0.0),
            jnp.where(merged == s_own, weight, 0.0),
            jnp.where(merged == s_own, 1.0, 0.0),
        )

    def col_ds(j, size):
        return pl.ds(pl.multiple_of(j * size, size), size)

    t_tile, s_tile = min(256, tw), min(256, sw)
    for load in loads[:2]:
        load.wait()

    @pl.loop(0, m_steps)
    def _(m):
        @pl.loop(0, tw // t_tile)
        def _(j):
            cols = col_ds(j, t_tile)
            x = tile_of(xg, m, pl.ds(0, width))
            g = jnp.dot(x, tg[:, cols], preferred_element_type=f32)
            u = jnp.dot(x, tu[:, cols], preferred_element_type=f32)
            th[row_ds(m), cols] = (g * jax.nn.sigmoid(g) * u).astype(bf16)

    for load in loads[2:4]:
        load.wait()

    @pl.loop(0, m_steps)
    def _(m):
        @pl.loop(0, sw // s_tile)
        def _(j):
            cols = col_ds(j, s_tile)
            _, _, keep = facts(m)
            x = tile_of(xg, m, pl.ds(0, width))
            g = jnp.dot(x, sg[:, cols], preferred_element_type=f32)
            u = jnp.dot(x, su[:, cols], preferred_element_type=f32)
            gate[row_ds(m), cols] = g
            up[row_ds(m), cols] = u
            sh[row_ds(m), cols] = (g * jax.nn.sigmoid(g) * u * keep).astype(bf16)

    for load in loads[4:]:
        load.wait()

    def fold(c, cols, stage):
        axis = ORDERS[c][2 - stage]
        done = ORDERS[c][: 2 - stage]
        buf = rbufs[3 * c + stage]
        copies = []
        for k in range(1, sizes[axis]):
            out = pltpu.make_async_remote_copy(
                src_ref=view(part, moved(axis, k), done, cols), dst_ref=buf.at[k - 1],
                send_sem=r_send.at[c, stage, k - 1], recv_sem=r_recv.at[c, stage, k - 1],
                device_id={"expert": number(moved(axis, k))}, device_id_type=MESH,
            )
            copies.append((out, out))
        return copies

    def total(c, cols, stage):
        done = ORDERS[c][: 2 - stage]
        place = region(at, done) + (pl.ds(0, SLOT), pl.ds(cols[0], cols[1] - cols[0]))
        value = part[place].astype(f32)
        for k in range(rbufs[3 * c + stage].shape[0]):
            value = value + rbufs[3 * c + stage][k].astype(f32)
        return place, value

    d_cols = bounds_of(width)
    folds = [[fold(c, d_cols[c], s) for s in range(3)] for c in range(len(ORDERS))]
    shares = [[spread(cot, c_send, c_recv, c, d_cols[c], s) for s in range(3)] for c in range(len(ORDERS))]
    for c, (low, high) in enumerate(d_cols):
        @pl.loop(0, m_steps)
        def _(m):
            @pl.loop(0, (high - low) // 256)
            def _(j):
                cols = pl.ds(pl.multiple_of(low + j * 256, 256), 256)
                t_scale, s_scale, _ = facts(m)
                value = jnp.dot(th[row_ds(m), :], td[:, cols], preferred_element_type=f32) * t_scale
                value += jnp.dot(sh[row_ds(m), :], sd[:, cols], preferred_element_type=f32) * s_scale
                part[pl.ds(m * y_tile, y_tile), :, :, :, cols] = value.astype(bf16).reshape(
                    y_tile, sx, sz, SLOT, 256
                )
        begin(folds[c][0])
    for s in (1, 2):
        for c in range(len(ORDERS)):
            arrive(folds[c][s - 1])
            place, value = total(c, d_cols[c], s - 1)
            part[place] = value.astype(bf16)
            begin(folds[c][s])
    own_weight = xg[region(at, ()) + (pl.ds(0, SLOT), pl.ds(width, EXTRA))].astype(f32)[..., 0:1]
    factor = 1.0 / math.sqrt(tok * count * 2)
    for c in range(len(ORDERS)):
        arrive(folds[c][2])
        place, value = total(c, d_cols[c], 2)
        cot[place] = (own_weight * value * factor).astype(bf16)
        begin(shares[c][0])
    for s in (1, 2):
        for c in range(len(ORDERS)):
            arrive(shares[c][s - 1])
            begin(shares[c][s])
    for c in range(len(ORDERS)):
        arrive(shares[c][2])
    outs.append(pltpu.make_async_copy(cot, cot_o, o_sem.at[1]))
    outs[1].start()

    other = 1 - core
    turned = (((0,), (0,)), ((), ()))

    @pl.loop(0, half // 256)
    def _(i):
        cols = pl.ds(pl.multiple_of(other * half + i * 256, 256), 256)
        value = jnp.zeros((sw, 256), f32)
        for m in range(m_steps):
            value += lax.dot_general(
                sh[row_ds(m), :], tile_of(cot, m, cols), turned, preferred_element_type=f32
            )
        td[pl.ds(0, sw), col_ds(i, 256)] = value.astype(bf16)

    def hand(i, src, dst):
        copy = pltpu.make_async_remote_copy(
            src_ref=src, dst_ref=dst, send_sem=g_send.at[i], recv_sem=g_recv.at[i],
            device_id={"dp": other}, device_id_type=MESH,
        )
        copy.start()
        return copy

    hands = [hand(0, td.at[pl.ds(0, sw), pl.ds(0, half)], got_down)]

    @pl.loop(0, m_steps)
    def _(m):
        @pl.loop(0, sw // s_tile)
        def _(j):
            cols = col_ds(j, s_tile)
            _, _, keep = facts(m)
            dh = lax.dot_general(
                tile_of(cot, m, pl.ds(0, width)), sd[cols, :], (((1,), (1,)), ((), ())),
                preferred_element_type=f32,
            ) * keep
            g, u = gate[row_ds(m), cols], up[row_ds(m), cols]
            s = jax.nn.sigmoid(g)
            dg[row_ds(m), cols] = (dh * u * s * (1.0 + g * (1.0 - s))).astype(bf16)
            du[row_ds(m), cols] = (dh * (g * s)).astype(bf16)

    for i, (src, dst) in enumerate(((dg, dg_o), (du, du_o), (sh, sh_o))):
        outs.append(pltpu.make_async_copy(src, dst, o_sem.at[2 + i]))
        outs[-1].start()

    for number_, (grad, got) in enumerate(((dg, got_gate), (du, got_up))):
        @pl.loop(0, half // 256)
        def _(i):
            cols = pl.ds(pl.multiple_of(other * half + i * 256, 256), 256)
            value = jnp.zeros((256, sw), f32)
            for m in range(m_steps):
                value += lax.dot_general(
                    tile_of(xg, m, cols), grad[row_ds(m), :], turned, preferred_element_type=f32
                )
            tg[col_ds(i, 256), pl.ds(number_ * sw, sw)] = value.astype(bf16)
        hands.append(hand(1 + number_, tg.at[pl.ds(0, half), pl.ds(number_ * sw, sw)], got))

    for c in range(len(ORDERS)):
        for s in range(3):
            left(plan[c][s])
            left(folds[c][s])
            left(shares[c][s])
    for copy in outs:
        copy.wait()
    for copy in hands:
        copy.wait()


def per_device(
    tokens, router_weight, initial_id, group_map,
    teacher_gate, teacher_up, teacher_down, student_gate, student_up, student_down,
):
    count = lax.axis_size("expert")
    sz = 4
    side = math.isqrt(count // sz)
    sizes = (side, side, sz)
    tok, width = tokens.shape
    half = width // 2
    rows = count * SLOT
    tw, sw = teacher_gate.shape[1], student_gate.shape[1]

    ids = initial_id[:, 0]
    merged = jnp.sum(
        jnp.where(ids[:, None] == jnp.arange(group_map.shape[0])[None, :], group_map[None, :], 0), axis=1
    )
    lane = jnp.arange(EXTRA)[None, :]
    extra = jnp.where(
        lane == 0, router_weight[:, None],
        jnp.where(lane == 1, ids[:, None].astype(bf16), merged[:, None].astype(bf16)),
    ).astype(bf16)
    block = jnp.pad(jnp.concatenate([tokens, extra], axis=1), ((0, SLOT - tok), (0, 0)))

    wide = sizes + (SLOT, width + EXTRA)
    narrow = sizes + (SLOT, width)
    out_shape = (
        jax.ShapeDtypeStruct((half, sw), bf16),
        jax.ShapeDtypeStruct((half, sw), bf16),
        jax.ShapeDtypeStruct((sw, half), bf16),
        jax.ShapeDtypeStruct(wide, bf16),
        jax.ShapeDtypeStruct(narrow, bf16),
        jax.ShapeDtypeStruct((rows, sw), bf16),
        jax.ShapeDtypeStruct((rows, sw), bf16),
        jax.ShapeDtypeStruct((rows, sw), bf16),
    )
    scratch = [
        pltpu.VMEM((width, tw), bf16), pltpu.VMEM((width, tw), bf16), pltpu.VMEM((tw, width), bf16),
        pltpu.VMEM((width, sw), bf16), pltpu.VMEM((width, sw), bf16), pltpu.VMEM((sw, width), bf16),
        pltpu.VMEM(wide, bf16), pltpu.VMEM(narrow, bf16), pltpu.VMEM(narrow, bf16),
        pltpu.VMEM((rows, sw), f32), pltpu.VMEM((rows, sw), f32),
        pltpu.VMEM((rows, tw), bf16), pltpu.VMEM((rows, sw), bf16),
        pltpu.VMEM((rows, sw), bf16), pltpu.VMEM((rows, sw), bf16),
        pltpu.SemaphoreType.DMA((6,)), pltpu.SemaphoreType.DMA((5,)),
        pltpu.SemaphoreType.DMA((3,)), pltpu.SemaphoreType.DMA((3,)),
    ] + [pltpu.SemaphoreType.DMA((len(ORDERS), 3, 3))] * 6
    for order, (low, high) in zip(ORDERS, bounds_of(width)):
        for stage in range(3):
            axis, done = order[2 - stage], order[: 2 - stage]
            dims = tuple(sizes[a] if a in done else 1 for a in (Y, X, Z))
            scratch.append(pltpu.VMEM((sizes[axis] - 1,) + dims + (SLOT, high - low), bf16))
    hbm = pl.BlockSpec(memory_space=pl.ANY)
    got_gate, got_up, got_down, xg, cot, dg, du, sh = pl.pallas_call(
        functools.partial(kernel, sizes, tok, width),
        out_shape=out_shape,
        in_specs=[pl.BlockSpec(memory_space=pltpu.VMEM)] + [hbm] * 6,
        out_specs=[hbm] * 8,
        scratch_shapes=scratch,
        compiler_params=pltpu.CompilerParams(
            collective_id=0, has_side_effects=True, vmem_limit_bytes=63 * 2**20
        ),
    )(block, teacher_gate, teacher_up, teacher_down, student_gate, student_up, student_down)

    start = lax.axis_index("dp") * half
    x_own = lax.dynamic_slice_in_dim(xg.reshape(rows, width + EXTRA), start, half, 1)
    c_own = lax.dynamic_slice_in_dim(cot.reshape(rows, width), start, half, 1)
    turned = (((0,), (0,)), ((), ()))

    def own(a, b, got):
        return lax.dot_general(a, b, turned, preferred_element_type=f32) + got.astype(f32)

    return own(x_own, dg, got_gate), own(x_own, du, got_up), own(sh, c_own, got_down)


def solution(mesh):
    placed = (
        P(("dp", "expert"), None),
        P(("dp", "expert")),
        P(("dp", "expert"), None),
        P(),
        P(None, "expert"),
        P(None, "expert"),
        P("expert", None),
        P(None, "expert"),
        P(None, "expert"),
        P("expert", None),
    )
    return jax.shard_map(
        per_device,
        mesh=mesh,
        in_specs=placed,
        out_specs=(P("dp", "expert"), P("dp", "expert"), P("expert", "dp")),
        check_vma=False,
    )
```

```python
import functools
import math

import jax
import jax.numpy as jnp
from jax import lax
from jax.experimental import pallas as pl
from jax.experimental.pallas import tpu as pltpu
from jax.sharding import PartitionSpec as P

F = 4096
SLOT = 16
EXTRA = 128
MESH = pl.DeviceIdType.MESH
Y, X, Z = 0, 1, 2
ORDERS = ((Z, X, Y), (Z, Y, X), (Z, X, Y), (Z, Y, X), (Z, X, Y))
PARTS = len(ORDERS)
bf16, f32 = jnp.bfloat16, jnp.float32


def pieces(width):
    step = width * 3 // 4 // PARTS
    return [(step * i, step * (i + 1)) for i in range(PARTS)]


def kernel(sizes, tok, width, *refs):
    (x_ref, tg_h, tu_h, td_h, sg_h, su_h, sd_h) = refs[:7]
    (got_gate, got_up, got_down, xg_o, cot_o, dg_o, du_o, sh_o) = refs[7:15]
    (tg, tu, td, sg, su, sd, xg, part, cot, gate, up, th, sh, dg, du, t_gate, t_up) = refs[15:32]
    (w_sem, o_sem, g_send, g_recv, a_send, a_recv, c_send, c_recv, r_send, r_recv) = refs[32:42]
    rbufs = refs[42:]
    sy, sx, sz = sizes
    count = sy * sx * sz
    rows = count * SLOT
    y_tile = max(1, 256 // (sx * sz * SLOT))
    m_rows = y_tile * sx * sz * SLOT
    m_steps = sy // y_tile
    tw, sw = tg.shape[1], sg.shape[1]
    half = width // 2
    sent = width * 3 // 4
    cut = width // 4 // PARTS

    me = lax.axis_index("expert")
    core = lax.axis_index("dp")
    at = [lax.rem(me // sx, sy), lax.rem(me, sx), me // (sx * sy)]

    def number(pos):
        return (pos[Z] * sy + pos[Y]) * sx + pos[X]

    def moved(axis, k):
        pos = list(at)
        pos[axis] = lax.rem(at[axis] + k + sizes[axis], sizes[axis])
        return pos

    loads = []
    for i, (src, dst) in enumerate(
        ((tg_h, tg), (tu_h, tu), (sg_h, sg), (su_h, su), (td_h, td), (sd_h, sd))
    ):
        loads.append(pltpu.make_async_copy(src, dst, w_sem.at[i]))
        loads[-1].start()

    barrier = pltpu.get_barrier_semaphore()
    for axis in (Y, X, Z):
        for k in range(1, sizes[axis]):
            pl.semaphore_signal(
                barrier, inc=1, device_id={"expert": number(moved(axis, k))}, device_id_type=MESH
            )
    pl.semaphore_signal(barrier, inc=1, device_id={"dp": 1 - core}, device_id_type=MESH)
    mine = (pl.ds(at[Y], 1), pl.ds(at[X], 1), pl.ds(at[Z], 1), pl.ds(0, SLOT))
    xg[mine + (pl.ds(0, sent),)] = x_ref[:, pl.ds(0, sent)].reshape(1, 1, 1, SLOT, sent)
    xg[mine + (pl.ds(width, EXTRA),)] = x_ref[:, pl.ds(sent, EXTRA)].reshape(1, 1, 1, SLOT, EXTRA)
    pl.semaphore_wait(barrier, sy + sx + sz - 2)

    def region(pos, done):
        return tuple(
            pl.ds(0, sizes[a]) if a in done else pl.ds(pos[a], 1) for a in (Y, X, Z)
        )

    def view(ref, pos, done, cols):
        return ref.at[region(pos, done) + (pl.ds(0, SLOT), pl.ds(cols[0], cols[1] - cols[0]))]

    def spread(buf, send, recv, c, cols, stage):
        axis, done = ORDERS[c % PARTS][stage], ORDERS[c % PARTS][:stage]
        copies = []
        for k in range(1, sizes[axis]):
            mine = view(buf, at, done, cols)
            out = pltpu.make_async_remote_copy(
                src_ref=mine, dst_ref=mine,
                send_sem=send.at[c, stage, k - 1], recv_sem=recv.at[c, stage, k - 1],
                device_id={"expert": number(moved(axis, k))}, device_id_type=MESH,
            )
            theirs = view(buf, moved(axis, -k), done, cols)
            came = pltpu.make_async_remote_copy(
                src_ref=theirs, dst_ref=theirs,
                send_sem=send.at[c, stage, k - 1], recv_sem=recv.at[c, stage, k - 1],
                device_id={"expert": number(moved(axis, -k))}, device_id_type=MESH,
            )
            copies.append((out, came))
        return copies

    def begin(copies):
        for out, _ in copies:
            out.start()

    def arrive(copies):
        for _, came in copies:
            came.wait_recv()

    def left(copies):
        for out, _ in copies:
            out.wait_send()

    def tile_of(ref, m, cols):
        got = ref[pl.ds(m * y_tile, y_tile), :, :, :, cols]
        return got.reshape(m_rows, got.shape[-1])

    def put_tile(ref, m, cols, value):
        ref[pl.ds(m * y_tile, y_tile), :, :, :, cols] = value.astype(bf16).reshape(
            y_tile, sx, sz, SLOT, value.shape[-1]
        )

    def row_ds(m):
        return pl.ds(pl.multiple_of(m * m_rows, m_rows), m_rows)

    def col_ds(j, size):
        return pl.ds(pl.multiple_of(j * size, size), size)

    def facts(m):
        extra = tile_of(xg, m, pl.ds(width, EXTRA)).astype(f32)
        weight, ids, merged = extra[:, 0:1], extra[:, 1:2], extra[:, 2:3]
        t_own = (me * tw // F).astype(f32)
        s_own = (me * sw // F).astype(f32)
        return (
            jnp.where(ids == t_own, -weight, 0.0),
            jnp.where(merged == s_own, weight, 0.0),
            jnp.where(merged == s_own, 1.0, 0.0),
        )

    cols_of = pieces(width)
    piece = cols_of[0][1]

    def rest_of(c):
        return pl.ds(sent + c * cut, cut)

    def place_in_slot(shape):
        return lax.broadcasted_iota(jnp.int32, shape, 0) % SLOT

    def unpack(ref, c):
        @pl.loop(0, m_steps)
        def _(m):
            where = place_in_slot((m_rows, cut)) // 4
            value = jnp.zeros((m_rows, cut), f32)
            for k in range(3):
                tile = tile_of(ref, m, pl.ds(cols_of[c][0] + k * cut, cut)).astype(f32)
                value = jnp.where(where == k, pltpu.roll(tile, m_rows - (12 - 4 * k), 0), value)
            put_tile(ref, m, rest_of(c), value)

    t_tile, s_tile = min(256, tw), min(256, sw)
    last = PARTS - 1

    def project(c, w_gate, w_up, g_sum, u_sum, hidden, size, tile, masked):
        @pl.loop(0, m_steps)
        def _(m):
            @pl.loop(0, size // tile)
            def _(j):
                cols = col_ds(j, tile)
                first = tile_of(xg, m, pl.ds(cols_of[c][0], piece))
                second = tile_of(xg, m, rest_of(c))

                def product(w):
                    return jnp.dot(
                        first, w[pl.ds(cols_of[c][0], piece), cols], preferred_element_type=f32
                    ) + jnp.dot(second, w[rest_of(c), cols], preferred_element_type=f32)

                g, u = product(w_gate), product(w_up)
                if c > 0:
                    g += g_sum[row_ds(m), cols]
                    u += u_sum[row_ds(m), cols]
                if c < last or masked:
                    g_sum[row_ds(m), cols] = g
                    u_sum[row_ds(m), cols] = u
                if c == last:
                    value = g * jax.nn.sigmoid(g) * u
                    if masked:
                        value = value * facts(m)[2]
                    hidden[row_ds(m), cols] = value.astype(bf16)

    x_cols = cols_of + [(width, width + EXTRA)]
    plan = [[spread(xg, a_send, a_recv, c, x_cols[c], s) for s in range(3)] for c in range(PARTS + 1)]
    begin(plan[PARTS][0])
    for c in range(PARTS):
        begin(plan[c][0])
    turn = [PARTS] + list(range(PARTS))
    for t in range(PARTS + 3):
        if 2 <= t < PARTS + 3:
            c = turn[t - 2]
            arrive(plan[c][1])
            begin(plan[c][2])
        if 0 <= t - 1 < PARTS + 1:
            c = turn[t - 1]
            arrive(plan[c][0])
            begin(plan[c][1])
        if 0 <= t - 3:
            c = turn[t - 3]
            arrive(plan[c][2])
            if c < PARTS:
                unpack(xg, c)
                if c == 0:
                    for load in loads[:4]:
                        load.wait()
                project(c, tg, tu, t_gate, t_up, th, tw, t_tile, False)
                project(c, sg, su, gate, up, sh, sw, s_tile, True)
    c = last
    arrive(plan[c][2])
    unpack(xg, c)
    outs = [pltpu.make_async_copy(xg, xg_o, o_sem.at[0])]
    outs[0].start()
    project(c, tg, tu, t_gate, t_up, th, tw, t_tile, False)
    project(c, sg, su, gate, up, sh, sw, s_tile, True)
    for load in loads[4:]:
        load.wait()

    def fold(c, cols, stage):
        axis = ORDERS[c][2 - stage]
        done = ORDERS[c][: 2 - stage]
        buf = rbufs[3 * c + stage]
        copies = []
        for k in range(1, sizes[axis]):
            out = pltpu.make_async_remote_copy(
                src_ref=view(part, moved(axis, k), done, cols), dst_ref=buf.at[k - 1],
                send_sem=r_send.at[c, stage, k - 1], recv_sem=r_recv.at[c, stage, k - 1],
                device_id={"expert": number(moved(axis, k))}, device_id_type=MESH,
            )
            copies.append((out, out))
        return copies

    def total(c, cols, stage):
        done = ORDERS[c][: 2 - stage]
        place = region(at, done) + (pl.ds(0, SLOT), pl.ds(cols[0], cols[1] - cols[0]))
        value = part[place].astype(f32)
        for k in range(rbufs[3 * c + stage].shape[0]):
            value = value + rbufs[3 * c + stage][k].astype(f32)
        return place, value

    folds = [[fold(c, cols_of[c], s) for s in range(3)] for c in range(PARTS)]
    shares = [[spread(cot, c_send, c_recv, c, cols_of[c], s) for s in range(3)] for c in range(PARTS)]
    factor = 1.0 / math.sqrt(tok * count * 2)

    def differ(c):
        @pl.loop(0, m_steps)
        def _(m):
            t_scale, s_scale, _ = facts(m)

            def tile(cols):
                value = jnp.dot(th[row_ds(m), :], td[:, cols], preferred_element_type=f32) * t_scale
                return value + jnp.dot(
                    sh[row_ds(m), :], sd[:, cols], preferred_element_type=f32
                ) * s_scale

            rest = tile(rest_of(c))
            where = place_in_slot((m_rows, cut))
            for k in range(3):
                cols = pl.ds(cols_of[c][0] + k * cut, cut)
                put_tile(part, m, cols, jnp.where(where >= 12, pltpu.roll(rest, 12 - 4 * k, 0), tile(cols)))

    def finish(c):
        own = xg[mine + (pl.ds(width, EXTRA),)].astype(f32).reshape(SLOT, EXTRA)[:, 0:1]
        own = jnp.broadcast_to(own, (SLOT, cut))
        where = place_in_slot((SLOT, cut))
        weight = jnp.concatenate(
            [jnp.where(where >= 12, pltpu.roll(own, 12 - 4 * k, 0), own) for k in range(3)], axis=1
        )
        place, value = total(c, cols_of[c], 2)
        value = weight * value.reshape(SLOT, piece) * factor
        cot[place] = value.astype(bf16).reshape(1, 1, 1, SLOT, piece)

    def back(c):
        @pl.loop(0, m_steps)
        def _(m):
            @pl.loop(0, sw // s_tile)
            def _(j):
                cols = col_ds(j, s_tile)
                nt = (((1,), (1,)), ((), ()))
                dh = lax.dot_general(
                    tile_of(cot, m, pl.ds(cols_of[c][0], piece)), sd[cols, pl.ds(cols_of[c][0], piece)],
                    nt, preferred_element_type=f32,
                ) + lax.dot_general(
                    tile_of(cot, m, rest_of(c)), sd[cols, rest_of(c)], nt, preferred_element_type=f32
                )
                if c > 0:
                    dh += t_gate[row_ds(m), cols]
                if c < last:
                    t_gate[row_ds(m), cols] = dh
                else:
                    dh = dh * facts(m)[2]
                    g, u = gate[row_ds(m), cols], up[row_ds(m), cols]
                    s = jax.nn.sigmoid(g)
                    dg[row_ds(m), cols] = (dh * u * s * (1.0 + g * (1.0 - s))).astype(bf16)
                    du[row_ds(m), cols] = (dh * (g * s)).astype(bf16)

    for t in range(PARTS + 6):
        if t < PARTS:
            differ(t)
            begin(folds[t][0])
        for late in (5, 4):
            if 0 <= t - late < PARTS:
                arrive(shares[t - late][late - 4])
                begin(shares[t - late][late - 3])
        if 0 <= t - 3 < PARTS:
            arrive(folds[t - 3][2])
            finish(t - 3)
            begin(shares[t - 3][0])
        for late in (2, 1):
            if 0 <= t - late < PARTS:
                c = t - late
                arrive(folds[c][late - 1])
                place, value = total(c, cols_of[c], late - 1)
                part[place] = value.astype(bf16)
                begin(folds[c][late])
        if 0 <= t - 6 < PARTS:
            arrive(shares[t - 6][2])
            unpack(cot, t - 6)
            back(t - 6)
    outs.append(pltpu.make_async_copy(cot, cot_o, o_sem.at[1]))
    outs[1].start()
    for i, (src, dst) in enumerate(((dg, dg_o), (du, du_o), (sh, sh_o))):
        outs.append(pltpu.make_async_copy(src, dst, o_sem.at[2 + i]))
        outs[-1].start()

    other = 1 - core
    turned = (((0,), (0,)), ((), ()))

    def hand(i, src, dst):
        copy = pltpu.make_async_remote_copy(
            src_ref=src, dst_ref=dst, send_sem=g_send.at[i], recv_sem=g_recv.at[i],
            device_id={"dp": other}, device_id_type=MESH,
        )
        copy.start()
        return copy

    hands = []
    for number_, (grad, got) in enumerate(((dg, got_gate), (du, got_up))):
        @pl.loop(0, half // 256)
        def _(i):
            cols = pl.ds(pl.multiple_of(other * half + i * 256, 256), 256)
            value = jnp.zeros((256, sw), f32)
            for m in range(m_steps):
                value += lax.dot_general(
                    tile_of(xg, m, cols), grad[row_ds(m), :], turned, preferred_element_type=f32
                )
            tg[col_ds(i, 256), pl.ds(number_ * sw, sw)] = value.astype(bf16)
        hands.append(hand(1 + number_, tg.at[pl.ds(0, half), pl.ds(number_ * sw, sw)], got))

    @pl.loop(0, half // 256)
    def _(i):
        cols = pl.ds(pl.multiple_of(other * half + i * 256, 256), 256)
        value = jnp.zeros((sw, 256), f32)
        for m in range(m_steps):
            value += lax.dot_general(
                sh[row_ds(m), :], tile_of(cot, m, cols), turned, preferred_element_type=f32
            )
        td[pl.ds(0, sw), col_ds(i, 256)] = value.astype(bf16)

    hands.append(hand(0, td.at[pl.ds(0, sw), pl.ds(0, half)], got_down))

    for s in range(3):
        for c in range(PARTS):
            left(folds[c][s])
            left(shares[c][s])
        for c in range(PARTS + 1):
            left(plan[c][s])
    for copy in outs:
        copy.wait()
    for copy in hands:
        copy.wait()


def per_device(
    tokens, router_weight, initial_id, group_map,
    teacher_gate, teacher_up, teacher_down, student_gate, student_up, student_down,
):
    count = lax.axis_size("expert")
    sz = 4
    side = math.isqrt(count // sz)
    sizes = (side, side, sz)
    tok, width = tokens.shape
    half = width // 2
    rows = count * SLOT
    tw, sw = teacher_gate.shape[1], student_gate.shape[1]

    ids = initial_id[:, 0]
    merged = jnp.sum(
        jnp.where(ids[:, None] == jnp.arange(group_map.shape[0])[None, :], group_map[None, :], 0), axis=1
    )
    lane = jnp.arange(EXTRA)[None, :]
    extra = jnp.where(
        lane == 0, router_weight[:, None],
        jnp.where(lane == 1, ids[:, None].astype(bf16), merged[:, None].astype(bf16)),
    ).astype(bf16)
    extra = jnp.pad(extra, ((0, SLOT - tok), (0, 0)), constant_values=-1)
    sent = width * 3 // 4
    cut = width // 4 // PARTS
    rest = tokens[:, sent:].reshape(3, 4, PARTS, cut).transpose(1, 2, 0, 3).reshape(4, sent)
    block = jnp.concatenate([jnp.concatenate([tokens[:, :sent], rest], axis=0), extra], axis=1)

    wide = sizes + (SLOT, width + EXTRA)
    narrow = sizes + (SLOT, width)
    out_shape = (
        jax.ShapeDtypeStruct((half, sw), bf16),
        jax.ShapeDtypeStruct((half, sw), bf16),
        jax.ShapeDtypeStruct((sw, half), bf16),
        jax.ShapeDtypeStruct(wide, bf16),
        jax.ShapeDtypeStruct(narrow, bf16),
        jax.ShapeDtypeStruct((rows, sw), bf16),
        jax.ShapeDtypeStruct((rows, sw), bf16),
        jax.ShapeDtypeStruct((rows, sw), bf16),
    )
    scratch = [
        pltpu.VMEM((width, tw), bf16), pltpu.VMEM((width, tw), bf16), pltpu.VMEM((tw, width), bf16),
        pltpu.VMEM((width, sw), bf16), pltpu.VMEM((width, sw), bf16), pltpu.VMEM((sw, width), bf16),
        pltpu.VMEM(wide, bf16), pltpu.VMEM(sizes + (SLOT, sent), bf16), pltpu.VMEM(narrow, bf16),
        pltpu.VMEM((rows, sw), f32), pltpu.VMEM((rows, sw), f32),
        pltpu.VMEM((rows, tw), bf16), pltpu.VMEM((rows, sw), bf16),
        pltpu.VMEM((rows, sw), bf16), pltpu.VMEM((rows, sw), bf16),
        pltpu.VMEM((rows, tw), f32), pltpu.VMEM((rows, tw), f32),
        pltpu.SemaphoreType.DMA((6,)), pltpu.SemaphoreType.DMA((5,)),
        pltpu.SemaphoreType.DMA((3,)), pltpu.SemaphoreType.DMA((3,)),
    ] + [pltpu.SemaphoreType.DMA((PARTS + 1, 3, 3))] * 6
    for order, (low, high) in zip(ORDERS, pieces(width)):
        for stage in range(3):
            axis, done = order[2 - stage], order[: 2 - stage]
            dims = tuple(sizes[a] if a in done else 1 for a in (Y, X, Z))
            scratch.append(pltpu.VMEM((sizes[axis] - 1,) + dims + (SLOT, high - low), bf16))
    hbm = pl.BlockSpec(memory_space=pl.ANY)
    got_gate, got_up, got_down, xg, cot, dg, du, sh = pl.pallas_call(
        functools.partial(kernel, sizes, tok, width),
        out_shape=out_shape,
        in_specs=[pl.BlockSpec(memory_space=pltpu.VMEM)] + [hbm] * 6,
        out_specs=[hbm] * 8,
        scratch_shapes=scratch,
        compiler_params=pltpu.CompilerParams(
            collective_id=0, has_side_effects=True, vmem_limit_bytes=63 * 2**20
        ),
    )(block, teacher_gate, teacher_up, teacher_down, student_gate, student_up, student_down)

    start = lax.axis_index("dp") * half
    x_own = lax.dynamic_slice_in_dim(xg.reshape(rows, width + EXTRA), start, half, 1)
    c_own = lax.dynamic_slice_in_dim(cot.reshape(rows, width), start, half, 1)
    turned = (((0,), (0,)), ((), ()))

    def own(a, b, got):
        return lax.dot_general(a, b, turned, preferred_element_type=f32) + got.astype(f32)

    return own(x_own, dg, got_gate), own(x_own, du, got_up), own(sh, c_own, got_down)


def solution(mesh):
    placed = (
        P(("dp", "expert"), None),
        P(("dp", "expert")),
        P(("dp", "expert"), None),
        P(),
        P(None, "expert"),
        P(None, "expert"),
        P("expert", None),
        P(None, "expert"),
        P(None, "expert"),
        P("expert", None),
    )
    return jax.shard_map(
        per_device,
        mesh=mesh,
        in_specs=placed,
        out_specs=(P("dp", "expert"), P("dp", "expert"), P("expert", "dp")),
        check_vma=False,
    )
```

```python
import functools
import math

import jax
import jax.numpy as jnp
from jax import lax
from jax.experimental import pallas as pl
from jax.experimental.pallas import tpu as pltpu
from jax.sharding import PartitionSpec as P

F = 4096
SLOT = 16
EXTRA = 128
MESH = pl.DeviceIdType.MESH
Y, X, Z = 0, 1, 2
ORDERS = ((X, Z, Y), (Y, Z, X), (Z, X, Y), (Z, Y, X), (Z, X, Y))
PARTS = len(ORDERS)
bf16, f32 = jnp.bfloat16, jnp.float32


def pieces(width):
    step = width * 3 // 4 // PARTS
    return [(step * i, step * (i + 1)) for i in range(PARTS)]


def kernel(sizes, tok, width, *refs):
    (x_ref, tg_h, tu_h, td_h, sg_h, su_h, sd_h) = refs[:7]
    (got_gate, got_up, got_down, xg_o, cot_o, dg_o, du_o, sh_o) = refs[7:15]
    (tg, tu, td, sg, su, sd, xg, part, cot, gate, up, th, sh, dg, du, t_gate, t_up) = refs[15:32]
    (w_sem, o_sem, g_send, g_recv, a_send, a_recv, c_send, c_recv, r_send, r_recv) = refs[32:42]
    rbufs = refs[42:]
    sy, sx, sz = sizes
    count = sy * sx * sz
    rows = count * SLOT
    y_tile = max(1, 256 // (sx * sz * SLOT))
    m_rows = y_tile * sx * sz * SLOT
    m_steps = sy // y_tile
    tw, sw = tg.shape[1], sg.shape[1]
    half = width // 2
    sent = width * 3 // 4
    cut = width // 4 // PARTS

    me = lax.axis_index("expert")
    core = lax.axis_index("dp")
    at = [lax.rem(me // sx, sy), lax.rem(me, sx), me // (sx * sy)]

    def number(pos):
        return (pos[Z] * sy + pos[Y]) * sx + pos[X]

    def moved(axis, k):
        pos = list(at)
        pos[axis] = lax.rem(at[axis] + k + sizes[axis], sizes[axis])
        return pos

    loads = []
    for i, (src, dst) in enumerate(
        ((tg_h, tg), (tu_h, tu), (sg_h, sg), (su_h, su), (td_h, td), (sd_h, sd))
    ):
        loads.append(pltpu.make_async_copy(src, dst, w_sem.at[i]))
        loads[-1].start()

    barrier = pltpu.get_barrier_semaphore()
    for axis in (Y, X, Z):
        for k in range(1, sizes[axis]):
            pl.semaphore_signal(
                barrier, inc=1, device_id={"expert": number(moved(axis, k))}, device_id_type=MESH
            )
    pl.semaphore_signal(barrier, inc=1, device_id={"dp": 1 - core}, device_id_type=MESH)
    mine = (pl.ds(at[Y], 1), pl.ds(at[X], 1), pl.ds(at[Z], 1), pl.ds(0, SLOT))
    xg[mine + (pl.ds(0, sent),)] = x_ref[:, pl.ds(0, sent)].reshape(1, 1, 1, SLOT, sent)
    xg[mine + (pl.ds(width, EXTRA),)] = x_ref[:, pl.ds(sent, EXTRA)].reshape(1, 1, 1, SLOT, EXTRA)
    pl.semaphore_wait(barrier, sy + sx + sz - 2)

    def region(pos, done):
        return tuple(
            pl.ds(0, sizes[a]) if a in done else pl.ds(pos[a], 1) for a in (Y, X, Z)
        )

    def view(ref, pos, done, cols):
        return ref.at[region(pos, done) + (pl.ds(0, SLOT), pl.ds(cols[0], cols[1] - cols[0]))]

    def spread(buf, send, recv, c, cols, stage):
        axis, done = ORDERS[c % PARTS][stage], ORDERS[c % PARTS][:stage]
        copies = []
        for k in range(1, sizes[axis]):
            mine = view(buf, at, done, cols)
            out = pltpu.make_async_remote_copy(
                src_ref=mine, dst_ref=mine,
                send_sem=send.at[c, stage, k - 1], recv_sem=recv.at[c, stage, k - 1],
                device_id={"expert": number(moved(axis, k))}, device_id_type=MESH,
            )
            theirs = view(buf, moved(axis, -k), done, cols)
            came = pltpu.make_async_remote_copy(
                src_ref=theirs, dst_ref=theirs,
                send_sem=send.at[c, stage, k - 1], recv_sem=recv.at[c, stage, k - 1],
                device_id={"expert": number(moved(axis, -k))}, device_id_type=MESH,
            )
            copies.append((out, came))
        return copies

    def begin(copies):
        for out, _ in copies:
            out.start()

    def arrive(copies):
        for _, came in copies:
            came.wait_recv()

    def left(copies):
        for out, _ in copies:
            out.wait_send()

    def tile_of(ref, m, cols):
        got = ref[pl.ds(m * y_tile, y_tile), :, :, :, cols]
        return got.reshape(m_rows, got.shape[-1])

    def put_tile(ref, m, cols, value):
        ref[pl.ds(m * y_tile, y_tile), :, :, :, cols] = value.astype(bf16).reshape(
            y_tile, sx, sz, SLOT, value.shape[-1]
        )

    def row_ds(m):
        return pl.ds(pl.multiple_of(m * m_rows, m_rows), m_rows)

    def col_ds(j, size):
        return pl.ds(pl.multiple_of(j * size, size), size)

    def facts(m):
        extra = tile_of(xg, m, pl.ds(width, EXTRA)).astype(f32)
        weight, ids, merged = extra[:, 0:1], extra[:, 1:2], extra[:, 2:3]
        t_own = (me * tw // F).astype(f32)
        s_own = (me * sw // F).astype(f32)
        return (
            jnp.where(ids == t_own, -weight, 0.0),
            jnp.where(merged == s_own, weight, 0.0),
            jnp.where(merged == s_own, 1.0, 0.0),
        )

    cols_of = pieces(width)
    piece = cols_of[0][1]

    def rest_of(c):
        return pl.ds(sent + c * cut, cut)

    def place_in_slot(shape):
        return lax.broadcasted_iota(jnp.int32, shape, 0) % SLOT

    def unpack(ref, c):
        @pl.loop(0, m_steps)
        def _(m):
            where = place_in_slot((m_rows, cut)) // 4
            value = jnp.zeros((m_rows, cut), f32)
            for k in range(3):
                tile = tile_of(ref, m, pl.ds(cols_of[c][0] + k * cut, cut)).astype(f32)
                value = jnp.where(where == k, pltpu.roll(tile, m_rows - (12 - 4 * k), 0), value)
            put_tile(ref, m, rest_of(c), value)

    t_tile, s_tile = min(256, tw), min(256, sw)
    last = PARTS - 1

    def project(c, w_gate, w_up, g_sum, u_sum, hidden, size, tile, masked):
        @pl.loop(0, m_steps)
        def _(m):
            @pl.loop(0, size // tile)
            def _(j):
                cols = col_ds(j, tile)
                first = tile_of(xg, m, pl.ds(cols_of[c][0], piece))
                second = tile_of(xg, m, rest_of(c))

                def product(w):
                    return jnp.dot(
                        first, w[pl.ds(cols_of[c][0], piece), cols], preferred_element_type=f32
                    ) + jnp.dot(second, w[rest_of(c), cols], preferred_element_type=f32)

                g, u = product(w_gate), product(w_up)
                if c > 0:
                    g += g_sum[row_ds(m), cols]
                    u += u_sum[row_ds(m), cols]
                if c < last or masked:
                    g_sum[row_ds(m), cols] = g
                    u_sum[row_ds(m), cols] = u
                if c == last:
                    value = g * jax.nn.sigmoid(g) * u
                    if masked:
                        value = value * facts(m)[2]
                    hidden[row_ds(m), cols] = value.astype(bf16)

    x_cols = cols_of + [(width, width + EXTRA)]
    plan = [[spread(xg, a_send, a_recv, c, x_cols[c], s) for s in range(3)] for c in range(PARTS + 1)]
    begin(plan[PARTS][0])
    for c in range(PARTS):
        begin(plan[c][0])
    turn = [PARTS] + list(range(PARTS))
    for t in range(PARTS + 3):
        if 2 <= t < PARTS + 3:
            c = turn[t - 2]
            arrive(plan[c][1])
            begin(plan[c][2])
        if 0 <= t - 1 < PARTS + 1:
            c = turn[t - 1]
            arrive(plan[c][0])
            begin(plan[c][1])
        if 0 <= t - 3:
            c = turn[t - 3]
            arrive(plan[c][2])
            if c < PARTS:
                unpack(xg, c)
                if c == 0:
                    for load in loads[:4]:
                        load.wait()
                project(c, tg, tu, t_gate, t_up, th, tw, t_tile, False)
                project(c, sg, su, gate, up, sh, sw, s_tile, True)
    c = last
    arrive(plan[c][2])
    unpack(xg, c)
    outs = [pltpu.make_async_copy(xg, xg_o, o_sem.at[0])]
    outs[0].start()
    project(c, tg, tu, t_gate, t_up, th, tw, t_tile, False)
    project(c, sg, su, gate, up, sh, sw, s_tile, True)
    for load in loads[4:]:
        load.wait()

    def fold(c, cols, stage):
        axis = ORDERS[c][2 - stage]
        done = ORDERS[c][: 2 - stage]
        buf = rbufs[3 * c + stage]
        copies = []
        for k in range(1, sizes[axis]):
            out = pltpu.make_async_remote_copy(
                src_ref=view(part, moved(axis, k), done, cols), dst_ref=buf.at[k - 1],
                send_sem=r_send.at[c, stage, k - 1], recv_sem=r_recv.at[c, stage, k - 1],
                device_id={"expert": number(moved(axis, k))}, device_id_type=MESH,
            )
            copies.append((out, out))
        return copies

    def total(c, cols, stage):
        done = ORDERS[c][: 2 - stage]
        place = region(at, done) + (pl.ds(0, SLOT), pl.ds(cols[0], cols[1] - cols[0]))
        value = part[place].astype(f32)
        for k in range(rbufs[3 * c + stage].shape[0]):
            value = value + rbufs[3 * c + stage][k].astype(f32)
        return place, value

    folds = [[fold(c, cols_of[c], s) for s in range(3)] for c in range(PARTS)]
    shares = [[spread(cot, c_send, c_recv, c, cols_of[c], s) for s in range(3)] for c in range(PARTS)]
    factor = 1.0 / math.sqrt(tok * count * 2)

    def differ(c):
        @pl.loop(0, m_steps)
        def _(m):
            t_scale, s_scale, _ = facts(m)

            def tile(cols):
                value = jnp.dot(th[row_ds(m), :], td[:, cols], preferred_element_type=f32) * t_scale
                return value + jnp.dot(
                    sh[row_ds(m), :], sd[:, cols], preferred_element_type=f32
                ) * s_scale

            rest = tile(rest_of(c))
            where = place_in_slot((m_rows, cut))
            for k in range(3):
                cols = pl.ds(cols_of[c][0] + k * cut, cut)
                put_tile(part, m, cols, jnp.where(where >= 12, pltpu.roll(rest, 12 - 4 * k, 0), tile(cols)))

    def finish(c):
        own = xg[mine + (pl.ds(width, EXTRA),)].astype(f32).reshape(SLOT, EXTRA)[:, 0:1]
        own = jnp.broadcast_to(own, (SLOT, cut))
        where = place_in_slot((SLOT, cut))
        weight = jnp.concatenate(
            [jnp.where(where >= 12, pltpu.roll(own, 12 - 4 * k, 0), own) for k in range(3)], axis=1
        )
        place, value = total(c, cols_of[c], 2)
        value = weight * value.reshape(SLOT, piece) * factor
        cot[place] = value.astype(bf16).reshape(1, 1, 1, SLOT, piece)

    def back(c):
        @pl.loop(0, m_steps)
        def _(m):
            @pl.loop(0, sw // s_tile)
            def _(j):
                cols = col_ds(j, s_tile)
                nt = (((1,), (1,)), ((), ()))
                dh = lax.dot_general(
                    tile_of(cot, m, pl.ds(cols_of[c][0], piece)), sd[cols, pl.ds(cols_of[c][0], piece)],
                    nt, preferred_element_type=f32,
                ) + lax.dot_general(
                    tile_of(cot, m, rest_of(c)), sd[cols, rest_of(c)], nt, preferred_element_type=f32
                )
                if c > 0:
                    dh += t_gate[row_ds(m), cols]
                if c < last:
                    t_gate[row_ds(m), cols] = dh
                else:
                    dh = dh * facts(m)[2]
                    g, u = gate[row_ds(m), cols], up[row_ds(m), cols]
                    s = jax.nn.sigmoid(g)
                    dg[row_ds(m), cols] = (dh * u * s * (1.0 + g * (1.0 - s))).astype(bf16)
                    du[row_ds(m), cols] = (dh * (g * s)).astype(bf16)

    for t in range(PARTS + 6):
        if t < PARTS:
            differ(t)
            begin(folds[t][0])
        for late in (5, 4):
            if 0 <= t - late < PARTS:
                arrive(shares[t - late][late - 4])
                begin(shares[t - late][late - 3])
        if 0 <= t - 3 < PARTS:
            arrive(folds[t - 3][2])
            finish(t - 3)
            begin(shares[t - 3][0])
        for late in (2, 1):
            if 0 <= t - late < PARTS:
                c = t - late
                arrive(folds[c][late - 1])
                place, value = total(c, cols_of[c], late - 1)
                part[place] = value.astype(bf16)
                begin(folds[c][late])
        if 0 <= t - 6 < PARTS:
            arrive(shares[t - 6][2])
            unpack(cot, t - 6)
            back(t - 6)
    outs.append(pltpu.make_async_copy(cot, cot_o, o_sem.at[1]))
    outs[1].start()
    for i, (src, dst) in enumerate(((dg, dg_o), (du, du_o), (sh, sh_o))):
        outs.append(pltpu.make_async_copy(src, dst, o_sem.at[2 + i]))
        outs[-1].start()

    other = 1 - core
    turned = (((0,), (0,)), ((), ()))

    def hand(i, src, dst):
        copy = pltpu.make_async_remote_copy(
            src_ref=src, dst_ref=dst, send_sem=g_send.at[i], recv_sem=g_recv.at[i],
            device_id={"dp": other}, device_id_type=MESH,
        )
        copy.start()
        return copy

    hands = []
    for number_, (grad, got) in enumerate(((dg, got_gate), (du, got_up))):
        @pl.loop(0, half // 256)
        def _(i):
            cols = pl.ds(pl.multiple_of(other * half + i * 256, 256), 256)
            value = jnp.zeros((256, sw), f32)
            for m in range(m_steps):
                value += lax.dot_general(
                    tile_of(xg, m, cols), grad[row_ds(m), :], turned, preferred_element_type=f32
                )
            tg[col_ds(i, 256), pl.ds(number_ * sw, sw)] = value.astype(bf16)
        hands.append(hand(1 + number_, tg.at[pl.ds(0, half), pl.ds(number_ * sw, sw)], got))

    @pl.loop(0, half // 256)
    def _(i):
        cols = pl.ds(pl.multiple_of(other * half + i * 256, 256), 256)
        value = jnp.zeros((sw, 256), f32)
        for m in range(m_steps):
            value += lax.dot_general(
                sh[row_ds(m), :], tile_of(cot, m, cols), turned, preferred_element_type=f32
            )
        td[pl.ds(0, sw), col_ds(i, 256)] = value.astype(bf16)

    hands.append(hand(0, td.at[pl.ds(0, sw), pl.ds(0, half)], got_down))

    for s in range(3):
        for c in range(PARTS):
            left(folds[c][s])
            left(shares[c][s])
        for c in range(PARTS + 1):
            left(plan[c][s])
    for copy in outs:
        copy.wait()
    for copy in hands:
        copy.wait()


def per_device(
    tokens, router_weight, initial_id, group_map,
    teacher_gate, teacher_up, teacher_down, student_gate, student_up, student_down,
):
    count = lax.axis_size("expert")
    sz = 4
    side = math.isqrt(count // sz)
    sizes = (side, side, sz)
    tok, width = tokens.shape
    half = width // 2
    rows = count * SLOT
    tw, sw = teacher_gate.shape[1], student_gate.shape[1]

    ids = initial_id[:, 0]
    merged = jnp.sum(
        jnp.where(ids[:, None] == jnp.arange(group_map.shape[0])[None, :], group_map[None, :], 0), axis=1
    )
    lane = jnp.arange(EXTRA)[None, :]
    extra = jnp.where(
        lane == 0, router_weight[:, None],
        jnp.where(lane == 1, ids[:, None].astype(bf16), merged[:, None].astype(bf16)),
    ).astype(bf16)
    extra = jnp.pad(extra, ((0, SLOT - tok), (0, 0)), constant_values=-1)
    sent = width * 3 // 4
    cut = width // 4 // PARTS
    rest = tokens[:, sent:].reshape(3, 4, PARTS, cut).transpose(1, 2, 0, 3).reshape(4, sent)
    block = jnp.concatenate([jnp.concatenate([tokens[:, :sent], rest], axis=0), extra], axis=1)

    wide = sizes + (SLOT, width + EXTRA)
    narrow = sizes + (SLOT, width)
    out_shape = (
        jax.ShapeDtypeStruct((half, sw), bf16),
        jax.ShapeDtypeStruct((half, sw), bf16),
        jax.ShapeDtypeStruct((sw, half), bf16),
        jax.ShapeDtypeStruct(wide, bf16),
        jax.ShapeDtypeStruct(narrow, bf16),
        jax.ShapeDtypeStruct((rows, sw), bf16),
        jax.ShapeDtypeStruct((rows, sw), bf16),
        jax.ShapeDtypeStruct((rows, sw), bf16),
    )
    scratch = [
        pltpu.VMEM((width, tw), bf16), pltpu.VMEM((width, tw), bf16), pltpu.VMEM((tw, width), bf16),
        pltpu.VMEM((width, sw), bf16), pltpu.VMEM((width, sw), bf16), pltpu.VMEM((sw, width), bf16),
        pltpu.VMEM(wide, bf16), pltpu.VMEM(sizes + (SLOT, sent), bf16), pltpu.VMEM(narrow, bf16),
        pltpu.VMEM((rows, sw), f32), pltpu.VMEM((rows, sw), f32),
        pltpu.VMEM((rows, tw), bf16), pltpu.VMEM((rows, sw), bf16),
        pltpu.VMEM((rows, sw), bf16), pltpu.VMEM((rows, sw), bf16),
        pltpu.VMEM((rows, tw), f32), pltpu.VMEM((rows, tw), f32),
        pltpu.SemaphoreType.DMA((6,)), pltpu.SemaphoreType.DMA((5,)),
        pltpu.SemaphoreType.DMA((3,)), pltpu.SemaphoreType.DMA((3,)),
    ] + [pltpu.SemaphoreType.DMA((PARTS + 1, 3, 3))] * 6
    for order, (low, high) in zip(ORDERS, pieces(width)):
        for stage in range(3):
            axis, done = order[2 - stage], order[: 2 - stage]
            dims = tuple(sizes[a] if a in done else 1 for a in (Y, X, Z))
            scratch.append(pltpu.VMEM((sizes[axis] - 1,) + dims + (SLOT, high - low), bf16))
    hbm = pl.BlockSpec(memory_space=pl.ANY)
    got_gate, got_up, got_down, xg, cot, dg, du, sh = pl.pallas_call(
        functools.partial(kernel, sizes, tok, width),
        out_shape=out_shape,
        in_specs=[pl.BlockSpec(memory_space=pltpu.VMEM)] + [hbm] * 6,
        out_specs=[hbm] * 8,
        scratch_shapes=scratch,
        compiler_params=pltpu.CompilerParams(
            collective_id=0, has_side_effects=True, vmem_limit_bytes=63 * 2**20
        ),
    )(block, teacher_gate, teacher_up, teacher_down, student_gate, student_up, student_down)

    start = lax.axis_index("dp") * half
    x_own = lax.dynamic_slice_in_dim(xg.reshape(rows, width + EXTRA), start, half, 1)
    c_own = lax.dynamic_slice_in_dim(cot.reshape(rows, width), start, half, 1)
    turned = (((0,), (0,)), ((), ()))

    def own(a, b, got):
        return lax.dot_general(a, b, turned, preferred_element_type=f32) + got.astype(f32)

    return own(x_own, dg, got_gate), own(x_own, du, got_up), own(sh, c_own, got_down)


def solution(mesh):
    placed = (
        P(("dp", "expert"), None),
        P(("dp", "expert")),
        P(("dp", "expert"), None),
        P(),
        P(None, "expert"),
        P(None, "expert"),
        P("expert", None),
        P(None, "expert"),
        P(None, "expert"),
        P("expert", None),
    )
    return jax.shard_map(
        per_device,
        mesh=mesh,
        in_specs=placed,
        out_specs=(P("dp", "expert"), P("dp", "expert"), P("expert", "dp")),
        check_vma=False,
    )
```
